32 devices in a mesh: blk: 8 (over y, x, core), col: 4 (over z).
Axes of the slice: x: 2, y: 2, z: 4, core: 2. Of those that a mesh axis runs over, the one named last changes fastest.
Arguments:
- three_index: float32 [4096, 12, 4096], P('blk', None, 'col'), may hold values from -6 to 6
- coefficients: float32 [4096, 1024], P('col', 'blk'), may hold values from -0.0078125 to 0.0078125
Outputs:
- exchange_matrix: float32 [4096, 4096], P(('blk', 'col'))
The draws below stay inside these ranges and needn't reach their ends.
All inputs are finite; a program needn't handle non-finite values.
Results may differ from the reference program's by a relative error of at most 0.000065.
Values sent between devices are 32-bit elements; how exact they have to be, the bound alone decides.
A program may use at most 128 MiB of HBM per device.

```python
import jax
import jax.numpy as jnp
from jax import lax

NBF = 4096
NOCC = 1024
AUX = 12


def steps_of(own_key, shape, cuts, least, high):
    def one(position, parts):
        draws = jax.random.uniform(jax.random.fold_in(jax.random.fold_in(own_key, 6), position), (parts,), jnp.float32, least / len(cuts), high / len(cuts))
        return jnp.repeat(jnp.exp(draws), shape[position] // parts).reshape((-1,) + (1,) * (len(shape) - position - 1))

    gain = one(*cuts[0])
    for cut in cuts[1:]:
        gain = gain * one(*cut)
    return gain


def centred(stream_key, dims, spread, bound, split=(), kind=jnp.bfloat16):
    result = jax.random.normal(stream_key, dims, jnp.float32) * spread
    if len(split) > 0:
        result = steps_of(stream_key, dims, split, -0.22, 0.18) * result
    return jnp.clip(result, min=-bound, max=bound).astype(kind)


def setup_inputs(seed: int = 0) -> dict:
    arg_keys = jax.random.split(jax.random.key(seed), 3)
    three_index = centred(arg_keys[0], (NBF, AUX, NBF), 1.0, 6.0, ((0, 8), (2, 4)), jnp.float32)
    coefficients = centred(arg_keys[1], (NBF, NOCC), (NBF * (AUX * NOCC) ** 0.5) ** -0.5, 0.0078125, ((0, 4), (1, 8)), jnp.float32)
    return {"three_index": three_index, "coefficients": coefficients}


def reference(three_index, coefficients):
    flattened = three_index.reshape(NBF * AUX, NBF)
    half_x = jnp.dot(flattened, coefficients, precision=lax.Precision.HIGHEST, preferred_element_type=jnp.float32)
    half_x = half_x.reshape(NBF, AUX * NOCC)
    return jnp.dot(half_x, half_x.T, precision=lax.Precision.HIGHEST, preferred_element_type=jnp.float32)
```

```python
import jax
import jax.numpy as jnp
from jax import lax
from jax.sharding import PartitionSpec as P

GROUPS = 6


def exchanged(block, axis, flip):
    route = [(i, i ^ flip) for i in range(lax.axis_size(axis))]
    return lax.ppermute(block, axis, route)


def product(left, right, dims):
    return lax.dot_general(
        left,
        right,
        (dims, ((), ())),
        precision=lax.Precision.HIGH,
        preferred_element_type=jnp.float32,
    )


def blocks_of_others(own, axis):
    count = lax.axis_size(axis)
    held = {0: own}
    far = [j for j in range(2, count, 2)]
    for j in far:
        if count == 8 and j == 6:
            half = own.shape[0] // 2
            first = exchanged(held[2][:half], axis, 4)
            second = exchanged(held[4][half:], axis, 2)
            held[6] = jnp.concatenate([first, second], axis=0)
        else:
            held[j] = exchanged(own, axis, j)
    for j in [0] + far:
        held[j + 1] = exchanged(held[j], axis, 1)
    return [held[j] for j in range(count)]


def on_device(three_index, coefficients):
    row_count, aux_count, _ = three_index.shape
    blk_size = lax.axis_size("blk")
    place = lax.axis_index("blk")
    orbitals = lax.all_gather(coefficients, "blk", axis=1, tiled=True)
    per_group = aux_count // GROUPS
    tiles = None
    for group in range(GROUPS):
        part = three_index[:, group * per_group : (group + 1) * per_group]
        partial_x = jnp.concatenate(
            [product(part[:, p], orbitals, ((1,), (0,))) for p in range(per_group)], axis=0
        )
        half_x = lax.psum_scatter(partial_x, "col", scatter_dimension=1, tiled=True)
        own = jnp.concatenate(
            [half_x[p * row_count : (p + 1) * row_count] for p in range(per_group)], axis=1
        )
        blocks = blocks_of_others(own, "blk")
        terms = [product(own, block, ((1,), (1,))) for block in blocks]
        tiles = terms if tiles is None else [t + u for t, u in zip(tiles, terms)]
    exchange_part = jnp.concatenate(tiles, axis=1)
    rows = lax.psum_scatter(exchange_part, "col", scatter_dimension=0, tiled=True)
    shares = jnp.split(rows, blk_size, axis=1)
    flip = 1
    while flip < blk_size:
        swap = (place & flip) != 0
        shares = [jnp.where(swap, shares[j ^ flip], shares[j]) for j in range(blk_size)]
        flip *= 2
    return jnp.concatenate(shares, axis=1)


def solution(mesh):
    return jax.shard_map(
        on_device,
        mesh=mesh,
        in_specs=(P("blk", None, "col"), P("col", "blk")),
        out_specs=P(("blk", "col"), None),
        check_vma=False,
    )
```

```python
import jax
import jax.numpy as jnp
from jax import lax
from jax.sharding import PartitionSpec as P

GROUPS = (2, 3, 3, 2, 1, 1)


def exchanged(block, axis, flip):
    route = [(i, i ^ flip) for i in range(lax.axis_size(axis))]
    return lax.ppermute(block, axis, route)


def product(left, right, dims):
    return lax.dot_general(
        left,
        right,
        (dims, ((), ())),
        precision=lax.Precision.HIGH,
        preferred_element_type=jnp.float32,
    )


def blocks_of_others(own, axis):
    count = lax.axis_size(axis)
    held = {0: own}
    far = [j for j in range(2, count, 2)]
    for j in far:
        if count == 8 and j == 6:
            half = own.shape[0] // 2
            first = exchanged(held[2][:half], axis, 4)
            second = exchanged(held[4][half:], axis, 2)
            held[6] = jnp.concatenate([first, second], axis=0)
        else:
            held[j] = exchanged(own, axis, j)
    for j in [0] + far:
        held[j + 1] = exchanged(held[j], axis, 1)
    return [held[j] for j in range(count)]


def on_device(three_index, coefficients):
    row_count, aux_count, _ = three_index.shape
    blk_size = lax.axis_size("blk")
    place = lax.axis_index("blk")
    orbitals = lax.all_gather(coefficients, "blk", axis=1, tiled=True)
    tiles = None
    earlier = []
    begin = 0
    for per_group in GROUPS:
        part = three_index[:, begin : begin + per_group]
        begin += per_group
        partial_x = jnp.concatenate(
            [product(part[:, p], orbitals, ((1,), (0,))) for p in range(per_group)], axis=0
        )
        if len(earlier) >= 2:
            partial_x, earlier[-2] = lax.optimization_barrier((partial_x, earlier[-2]))
        half_x = lax.psum_scatter(partial_x, "col", scatter_dimension=1, tiled=True)
        if len(earlier) >= 2:
            tiles = [t + u for t, u in zip(tiles, earlier[-2])] if tiles else earlier[-2]
        if earlier:
            half_x, earlier[-1] = lax.optimization_barrier((half_x, earlier[-1]))
        own = jnp.concatenate(
            [half_x[p * row_count : (p + 1) * row_count] for p in range(per_group)], axis=1
        )
        blocks = blocks_of_others(own, "blk")
        earlier.append([product(own, block, ((1,), (1,))) for block in blocks])
    for terms in earlier[-2:]:
        tiles = [t + u for t, u in zip(tiles, terms)]
    exchange_part = jnp.concatenate(tiles, axis=1)
    rows = lax.psum_scatter(exchange_part, "col", scatter_dimension=0, tiled=True)
    shares = jnp.split(rows, blk_size, axis=1)
    flip = 1
    while flip < blk_size:
        swap = (place & flip) != 0
        shares = [jnp.where(swap, shares[j ^ flip], shares[j]) for j in range(blk_size)]
        flip *= 2
    return jnp.concatenate(shares, axis=1)


def solution(mesh):
    return jax.shard_map(
        on_device,
        mesh=mesh,
        in_specs=(P("blk", None, "col"), P("col", "blk")),
        out_specs=P(("blk", "col"), None),
        check_vma=False,
    )
```

```python
import jax
import jax.numpy as jnp
from jax import lax
from jax.sharding import PartitionSpec as P

GROUPS = (1, 3, 3, 2, 1, 1, 1)


def exchanged(block, axis, flip):
    route = [(i, i ^ flip) for i in range(lax.axis_size(axis))]
    return lax.ppermute(block, axis, route)


def product(left, right, dims):
    return lax.dot_general(
        left,
        right,
        (dims, ((), ())),
        precision=lax.Precision.HIGH,
        preferred_element_type=jnp.float32,
    )


def blocks_of_others(own, axis):
    count = lax.axis_size(axis)
    held = {0: own}
    far = [j for j in range(2, count, 2)]
    for j in far:
        if count == 8 and j == 6:
            half = own.shape[0] // 2
            first = exchanged(held[2][:half], axis, 4)
            second = exchanged(held[4][half:], axis, 2)
            held[6] = jnp.concatenate([first, second], axis=0)
        else:
            held[j] = exchanged(own, axis, j)
    for j in [0] + far:
        held[j + 1] = exchanged(held[j], axis, 1)
    return [held[j] for j in range(count)]


def on_device(three_index, coefficients):
    row_count, aux_count, _ = three_index.shape
    blk_size = lax.axis_size("blk")
    place = lax.axis_index("blk")
    width = coefficients.shape[1]
    orbitals = jnp.zeros((coefficients.shape[0], width * blk_size), jnp.float32)
    for j, block in enumerate(blocks_of_others(coefficients, "blk")):
        orbitals = lax.dynamic_update_slice(orbitals, block, (0, (place ^ j) * width))
    tiles = None
    earlier = []
    begin = 0
    for per_group in GROUPS:
        part = three_index[:, begin : begin + per_group]
        begin += per_group
        partial_x = jnp.concatenate(
            [product(part[:, p], orbitals, ((1,), (0,))) for p in range(per_group)], axis=0
        )
        if len(earlier) >= 3:
            partial_x, earlier[-3] = lax.optimization_barrier((partial_x, earlier[-3]))
        half_x = lax.psum_scatter(partial_x, "col", scatter_dimension=1, tiled=True)
        if len(earlier) >= 3:
            tiles = [t + u for t, u in zip(tiles, earlier[-3])] if tiles else earlier[-3]
        if earlier:
            half_x, earlier[-1] = lax.optimization_barrier((half_x, earlier[-1]))
        own = jnp.concatenate(
            [half_x[p * row_count : (p + 1) * row_count] for p in range(per_group)], axis=1
        )
        blocks = blocks_of_others(own, "blk")
        earlier.append([product(own, block, ((1,), (1,))) for block in blocks])
    for terms in earlier[-3:]:
        tiles = [t + u for t, u in zip(tiles, terms)]
    exchange_part = jnp.concatenate(tiles, axis=1)
    rows = lax.psum_scatter(exchange_part, "col", scatter_dimension=0, tiled=True)
    shares = jnp.split(rows, blk_size, axis=1)
    flip = 1
    while flip < blk_size:
        swap = (place & flip) != 0
        shares = [jnp.where(swap, shares[j ^ flip], shares[j]) for j in range(blk_size)]
        flip *= 2
    return jnp.concatenate(shares, axis=1)


def solution(mesh):
    return jax.shard_map(
        on_device,
        mesh=mesh,
        in_specs=(P("blk", None, "col"), P("col", "blk")),
        out_specs=P(("blk", "col"), None),
        check_vma=False,
    )
```

```python
import jax
import jax.numpy as jnp
from jax import lax
from jax.sharding import PartitionSpec as P

GROUPS = (1, 3, 3, 2, 1, 1, 1)


def exchanged(block, axis, flip):
    route = [(i, i ^ flip) for i in range(lax.axis_size(axis))]
    return lax.ppermute(block, axis, route)


def product(left, right, dims):
    return lax.dot_general(
        left,
        right,
        (dims, ((), ())),
        precision=lax.Precision.HIGH,
        preferred_element_type=jnp.float32,
    )


def blocks_of_others(own, axis):
    count = lax.axis_size(axis)
    held = {0: own}
    far = [j for j in range(2, count, 2)]
    for j in far:
        if count == 8 and j == 6:
            half = own.shape[0] // 2
            first = exchanged(held[2][:half], axis, 4)
            second = exchanged(held[4][half:], axis, 2)
            held[6] = jnp.concatenate([first, second], axis=0)
        else:
            held[j] = exchanged(own, axis, j)
    for j in [0] + far:
        held[j + 1] = exchanged(held[j], axis, 1)
    return [held[j] for j in range(count)]


def in_order(parts, index):
    flip = 1
    while flip < len(parts):
        swap = (index & flip) != 0
        parts = [jnp.where(swap, parts[j ^ flip], parts[j]) for j in range(len(parts))]
        flip *= 2
    return parts


def side(index, j):
    return (index >> (j.bit_length() - 1)) & 1


def gram_tiles(own, blocks, place):
    half = own.shape[0] // 2
    tiles = [product(own, own, ((1,), (1,)))]
    for j in range(1, len(blocks)):
        for r in range(2):
            start = (side(place, j) ^ r) * half
            other = lax.dynamic_slice_in_dim(blocks[j], start, half, axis=0)
            tiles.append(product(own[r * half : (r + 1) * half], other, ((1,), (1,))))
    return tiles


def mirrored(rows, row_count, place):
    blk_size, col_size = lax.axis_size("blk"), lax.axis_size("col")
    half, share, pieces = row_count // 2, row_count // col_size, col_size // 2
    col = lax.axis_index("col")
    high, low = col // pieces, col % pieces
    flipped = rows[:, row_count:].T
    blocks = [rows[:, :row_count]]
    for j in range(1, blk_size):
        got = []
        for t in range(pieces):
            route = []
            for b in range(blk_size):
                for c in range(col_size):
                    target = ((c // pieces) ^ side(b, j)) * pieces + ((c % pieces) ^ t)
                    route.append((b * col_size + c, (b ^ j) * col_size + target))
            piece = lax.dynamic_slice_in_dim(
                flipped, (j - 1) * half + (low ^ t) * share, share, axis=0
            )
            got.append(lax.ppermute(piece, ("blk", "col"), route))
        other = jnp.concatenate(in_order(got, low), axis=1)
        mine = rows[:, row_count + (j - 1) * half : row_count + j * half]
        blocks.append(jnp.concatenate(in_order([mine, other], high ^ side(place, j)), axis=1))
    return jnp.concatenate(in_order(blocks, place), axis=1)


def on_device(three_index, coefficients):
    row_count, aux_count, _ = three_index.shape
    blk_size = lax.axis_size("blk")
    place = lax.axis_index("blk")
    width = coefficients.shape[1]
    orbitals = jnp.zeros((coefficients.shape[0], width * blk_size), jnp.float32)
    for j, block in enumerate(blocks_of_others(coefficients, "blk")):
        orbitals = lax.dynamic_update_slice(orbitals, block, (0, (place ^ j) * width))
    tiles = None
    earlier = []
    begin = 0
    for per_group in GROUPS:
        part = three_index[:, begin : begin + per_group]
        begin += per_group
        partial_x = jnp.concatenate(
            [product(part[:, p], orbitals, ((1,), (0,))) for p in range(per_group)], axis=0
        )
        if len(earlier) >= 3:
            partial_x, earlier[-3] = lax.optimization_barrier((partial_x, earlier[-3]))
        half_x = lax.psum_scatter(partial_x, "col", scatter_dimension=1, tiled=True)
        if len(earlier) >= 3:
            tiles = [t + u for t, u in zip(tiles, earlier[-3])] if tiles else earlier[-3]
        if earlier:
            half_x, earlier[-1] = lax.optimization_barrier((half_x, earlier[-1]))
        own = jnp.concatenate(
            [half_x[p * row_count : (p + 1) * row_count] for p in range(per_group)], axis=1
        )
        blocks = blocks_of_others(own, "blk")
        earlier.append(gram_tiles(own, blocks, place))
    for terms in earlier[-3:]:
        tiles = [t + u for t, u in zip(tiles, terms)]
    stacked = [
        jnp.concatenate(tiles[2 * j - 1 : 2 * j + 1], axis=0) for j in range(1, blk_size)
    ]
    exchange_part = jnp.concatenate([tiles[0]] + stacked, axis=1)
    rows = lax.psum_scatter(exchange_part, "col", scatter_dimension=0, tiled=True)
    return mirrored(rows, row_count, place)


def solution(mesh):
    return jax.shard_map(
        on_device,
        mesh=mesh,
        in_specs=(P("blk", None, "col"), P("col", "blk")),
        out_specs=P(("blk", "col"), None),
        check_vma=False,
    )
```
